512 devices in a mesh: rows: 128 (over y, z, core), rep: 4 (over x).
Axes of the slice: x: 4, y: 8, z: 8, core: 2. Of those that a mesh axis runs over, the one named last changes fastest.
Arguments:
- embeddings: bfloat16 [32768, 1024], P('rows', 'rep'), may hold values from -6 to 6
- coarse_ids: int32 [32768], P('rows'), may hold values from 0 to 255
- fine_ids: int32 [32768], P('rows'), may hold values from 0 to 65535, as said below
- pq_codes: int32 [32768, 64], P('rows', 'rep'), may hold values from 0 to 255
- old_coarse: float32 [256, 1024], P(None, 'rep'), may hold values from -3 to 3
- old_fine: float32 [65536, 1024], P('rows', 'rep'), may hold values from -3 to 3
- old_codebook: float32 [256, 1024], P('rows', 'rep'), may hold values from -3 to 3
Outputs:
- new_coarse: float32 [256, 1024], P(None, 'rep')
- new_fine: float32 [65536, 1024], P('rows', 'rep')
- residual: bfloat16 [32768, 1024], P('rows', 'rep')
- new_codebook: float32 [256, 1024], P('rows', 'rep')
- row_error: float32 [32768], P('rows')
The draws below stay inside these ranges and needn't reach their ends.
Inputs may be any that keep to these rules, and one draw needn't show every extreme that they name: `fine_ids`: within each aligned block of 256 rows, at most 8 ids lie in any one range o * 512 to (o + 1) * 512 - 1, and in every block some range holds exactly 8 of them.
All inputs are finite; a program needn't handle non-finite values.
Results may differ from the reference program's by a relative error of at most 0.0049.
Values may be sent and summed in bfloat16 or wider, within the bound.
A program may use at most 64 MiB of HBM per device.

```python
import math
import jax
import jax.numpy as jnp
import numpy as np
from jax import lax

D = 1024
NCOARSE = 256
NFINE = 65536
M = 64
KSUB = 256
ROW_DEV = 256
DSUB = 16
NROWS = 32768
FINE_DEV = 512
CAP = 8
N_ROWS = 128


def draw_fine_ids(key, part):
    base = jax.random.fold_in(key, 11)
    random_keys = jax.random.split(base, 7)
    owner_rows = N_ROWS
    candidate_count = owner_rows * CAP
    heavy_total = max(1, owner_rows // 16)
    order = jax.random.permutation(random_keys[0], owner_rows)
    heavy_clusters = jnp.zeros((owner_rows,), jnp.int32).at[order[:heavy_total]].set(1)
    noise_extra = jax.random.randint(random_keys[1], (N_ROWS, owner_rows), 0, 2)
    extra_score = jnp.where(heavy_clusters[None, :] == 1, 3, noise_extra)
    owner_of_slot = jnp.arange(candidate_count, dtype=jnp.int32) // CAP
    random_portion = jax.random.randint(random_keys[2], (N_ROWS, candidate_count), 0, 4096)
    owner_scores = (extra_score[:, owner_of_slot] * 4096 + random_portion) * candidate_count + jnp.arange(candidate_count, dtype=jnp.int32)[None, :]
    _, chosen = lax.top_k(owner_scores, ROW_DEV)
    chosen = jax.random.permutation(random_keys[3], chosen, axis=1, independent=True)
    owner_ids = chosen // CAP
    first = jax.random.randint(random_keys[4], (N_ROWS, ROW_DEV), 0, FINE_DEV)
    second = jax.random.randint(random_keys[5], (N_ROWS, ROW_DEV), 0, FINE_DEV)
    offsets = jax.random.randint(random_keys[6], (owner_rows,), 0, FINE_DEV)
    local_ids = (first * second // FINE_DEV + offsets[owner_ids]) % FINE_DEV
    return (owner_ids * FINE_DEV + local_ids).reshape(-1).astype(jnp.int32)


def set_ends(array, key, low, high):
    place = [jax.random.randint(jax.random.fold_in(key, axis), (), 0, length) for axis, length in enumerate(array.shape)]
    main_axis = array.shape.index(max(array.shape))
    beside = place[:main_axis] + [(place[main_axis] + 1) % array.shape[main_axis]] + place[main_axis + 1:]
    return array.at[tuple(place)].set(low).at[tuple(beside)].set(high)


def steps_of(stream_key, extent, shards, smallest, largest):
    loudness, own = 1.0, jax.random.fold_in(stream_key, 6)
    for axis_at, blocks in shards:
        steps = jnp.exp(jax.random.uniform(jax.random.fold_in(own, axis_at), (blocks,), jnp.float32, smallest / len(shards), largest / len(shards)))
        loudness = loudness * jnp.repeat(steps, extent[axis_at] // blocks).reshape([-1 if axis == axis_at else 1 for axis in range(len(extent))])
    return loudness


def rank_bounds(amount, skew):
    portions = [(1 << 20) // math.isqrt(standing ** skew) + 1 for standing in range(1, amount + 1)]
    spread = 1 + sum(portions) // (1 << 30)
    return np.cumsum(np.array([max(1, weight // spread) for weight in portions]))


def skewed_ids(key, shape, number_of, lean):
    grid = rank_bounds(number_of, lean)
    lot = jax.random.randint(jax.random.fold_in(key, 1), shape, 0, int(grid[number_of - 1]))
    rank = jnp.searchsorted(jnp.asarray(grid, jnp.int32), lot, side="right")
    return jax.random.permutation(jax.random.fold_in(key, 2), number_of)[rank].astype(jnp.int32)


def scatter_about(own_key, shape, deviation, bound, cuts=(), kind=jnp.bfloat16):
    values = deviation * jax.random.normal(own_key, shape, jnp.float32)
    if cuts:
        values = values * steps_of(own_key, shape, cuts, -0.22, 0.18)
    return jnp.clip(values, -bound, bound).astype(kind)


def setup_inputs(seed: int = 0) -> dict:
    streams_of = jax.random.split(jax.random.key(seed), 8)
    embeddings = scatter_about(streams_of[0], (NROWS, D), 1.0, 6.0, ((0, 128), (1, 4)))
    coarse_ids = set_ends(skewed_ids(streams_of[1], (NROWS,), NCOARSE, 4), jax.random.fold_in(streams_of[1], 3), 0, NCOARSE - 1).astype(jnp.int32)
    fine_ids = draw_fine_ids(jax.random.fold_in(streams_of[7], 71), 0)
    pq_codes = set_ends(skewed_ids(streams_of[3], (NROWS, M), KSUB, 4), jax.random.fold_in(streams_of[3], 3), 0, KSUB - 1).astype(jnp.int32)
    old_coarse = scatter_about(streams_of[4], (NCOARSE, D), 0.5, 3.0, ((1, 4),), jnp.float32)
    old_fine = scatter_about(streams_of[5], (NFINE, D), 0.5, 3.0, ((0, 128), (1, 4)), jnp.float32)
    old_codebook = scatter_about(streams_of[6], (KSUB, D), 0.5, 3.0, ((0, 128), (1, 4)), jnp.float32)
    return dict(embeddings=embeddings, coarse_ids=coarse_ids, fine_ids=fine_ids, pq_codes=pq_codes, old_coarse=old_coarse, old_fine=old_fine, old_codebook=old_codebook)


def update_means(sums, counts, fallback):
    return jnp.where(counts[:, None] > 0, sums / jnp.maximum(counts, 1.0)[:, None], fallback)


def reference(embeddings, coarse_ids, fine_ids, pq_codes, old_coarse, old_fine, old_codebook):
    ones_rows = jnp.ones((NROWS,), jnp.float32)
    coarse_sum = jax.ops.segment_sum(embeddings.astype(jnp.float32), coarse_ids, num_segments=NCOARSE)
    coarse_count = jax.ops.segment_sum(ones_rows, coarse_ids, num_segments=NCOARSE)
    new_coarse = update_means(coarse_sum, coarse_count, old_coarse)
    coarse_residual = (embeddings.astype(jnp.float32) - new_coarse[coarse_ids]).astype(jnp.bfloat16)
    fine_sum = jax.ops.segment_sum(coarse_residual.astype(jnp.float32), fine_ids, num_segments=NFINE)
    fine_count = jax.ops.segment_sum(ones_rows, fine_ids, num_segments=NFINE)
    new_fine = update_means(fine_sum, fine_count, old_fine)
    residual = (coarse_residual.astype(jnp.float32) - new_fine[fine_ids]).astype(jnp.bfloat16)
    pieces = residual.astype(jnp.float32).reshape(NROWS, M, DSUB)
    segment_ids = (pq_codes + KSUB * jnp.arange(M, dtype=jnp.int32)[None, :]).astype(jnp.int32)
    code_sum = jax.ops.segment_sum(pieces.reshape(NROWS * M, DSUB), segment_ids.reshape(-1), num_segments=M * KSUB)
    code_sum = code_sum.reshape(M, KSUB, DSUB)
    code_count = jax.ops.segment_sum(jnp.ones((NROWS * M,), jnp.float32), segment_ids.reshape(-1), num_segments=M * KSUB)
    code_count = code_count.reshape(M, KSUB)
    old_view = old_codebook.reshape(KSUB, M, DSUB).transpose(1, 0, 2)
    book_means = jnp.where(code_count[:, :, None] > 0, code_sum / jnp.maximum(code_count, 1.0)[:, :, None], old_view)
    rebuilt = book_means[jnp.arange(M, dtype=jnp.int32)[None, :], pq_codes]
    differ = pieces - rebuilt
    row_error = jnp.sum(differ * differ, axis=(1, 2)) / D
    new_codebook = book_means.transpose(1, 0, 2).reshape(KSUB, D)
    return new_coarse, new_fine, residual, new_codebook, row_error
```

```python
import functools

import jax
import jax.numpy as jnp
from jax import lax
from jax.experimental import pallas as pl
from jax.experimental.pallas import tpu as pltpu
from jax.sharding import Mesh
from jax.sharding import PartitionSpec as P

MESH = pl.DeviceIdType.MESH
ROWS = ("ry", "rz", "rc")
F32, BF16, I32 = jnp.float32, jnp.bfloat16, jnp.int32
LANES = 128


def iota(shape, dim):
    return lax.broadcasted_iota(I32, shape, dim)


def hot(cond):
    return jnp.where(cond, 1.0, 0.0).astype(BF16)


def dot(a, b):
    return jnp.dot(a, b, preferred_element_type=F32)


def parts(a, count):
    out = []
    for _ in range(count):
        p = a.astype(BF16)
        out.append(p)
        a = a - p.astype(F32)
    return out


def kernel(cfg, emb, cids, fids, pq, old_coarse, old_fine, old_book,
           o_coarse, o_fine, o_res, o_book, o_err,
           xs, xr, ms, mr, bs, br,
           in1, core1, rs1, x1, full1,
           in2, core2, rs2, x2, full2,
           err, s_send, s_x, s_m, s_b, s_ar1, s_ar2, s_e):
    Y, Z, C, X = cfg["Y"], cfg["Z"], cfg["C"], cfg["X"]
    R, n, W, cap, fine_dev, K, sub = (cfg[k] for k in ("R", "n", "W", "cap", "fine_dev", "K", "sub"))
    S, half, TR, sw = R * cap, K // 2, K // 2 // (Y + Z), W // sub
    groups = cfg["groups"]
    src_g, slots_g = R // groups, S // groups
    y, z, c, x = (lax.axis_index(a) for a in (*ROWS, "rep"))

    def at(dy=0, dz=0, dc=0, dx=0):
        return {
            "ry": lax.rem(y + dy, Y),
            "rz": lax.rem(z + dz, Z),
            "rc": lax.rem(c + dc, C),
            "rep": lax.rem(x + dx, X),
        }

    def offset(d):
        return at(d // (Z * C), lax.rem(d // C, Z), lax.rem(d, C))

    def back(d):
        dy, dz, dc = d // (Z * C), lax.rem(d // C, Z), lax.rem(d, C)
        return lax.rem(Y - dy, Y) * (Z * C) + lax.rem(Z - dz, Z) * C + lax.rem(C - dc, C)

    def remote(src, dst, recv, where, send):
        return pltpu.make_async_remote_copy(src, dst, send, recv, device_id=where, device_id_type=MESH)

    def arrived(ref, sem):
        pltpu.make_async_copy(ref, ref, sem).wait()

    gate = pltpu.get_barrier_semaphore()

    def greet(d, _):
        pl.semaphore_signal(gate, inc=1, device_id=offset(d), device_id_type=MESH)
        return 0

    lax.fori_loop(1, R, greet, 0)
    for d in range(1, X):
        pl.semaphore_signal(gate, inc=1, device_id=at(dx=d), device_id_type=MESH)

    cid_r, fid_r = cids[...], fids[...]
    own = fid_r // fine_dev
    loc = fid_r - own * fine_dev
    coarse_hot = hot(iota((K, n), 0) == cid_r)
    ones_lane = lambda lane: hot(iota((n, LANES), 1) == lane)
    pq16 = pq[...].astype(F32).astype(BF16)
    spread = hot((iota((sub, cap * sub), 1) & (sub - 1)) == iota((sub, cap * sub), 0))
    pq_wide = dot(pq16, spread)
    in1[:, :, :, :W] = dot(coarse_hot, emb[...]).reshape(2, Y + Z, TR, W)
    pq_rows = jnp.transpose(pq_wide[:, :LANES])
    tally = dot(coarse_hot, ones_lane(sub))
    for m in range(sub):
        tally += dot(hot(iota((K, n), 0).astype(F32) == pq_rows[m : m + 1, :]), ones_lane(m))
    in1[:, :, :, W:] = tally.reshape(2, Y + Z, TR, LANES)

    rel_r = (
        ((own // (Z * C) - y) & (Y - 1)) * (Z * C) + (((own // C) - z) & (Z - 1)) * C + ((own - c) & (C - 1))
    ).astype(F32)
    same = iota((n, n), 0) == iota((n, n), 1)

    def column(row):
        return jnp.sum(jnp.where(same, row, 0.0), axis=1, keepdims=True)

    rel_c, cid_c, loc_c = column(rel_r), column(cid_r.astype(F32)), column(loc.astype(F32))
    eq = rel_c == rel_r
    before = iota((n, n), 0) < iota((n, n), 1)
    after = iota((n, n), 0) > iota((n, n), 1)
    rank_r = jnp.sum(jnp.where(eq & before, 1.0, 0.0), axis=0, keepdims=True)
    rank_c = jnp.sum(jnp.where(eq & after, 1.0, 0.0), axis=1, keepdims=True)
    slot_r = rel_r * cap + rank_r
    slot_c = rel_c * cap + rank_c
    for g in range(groups):
        pick = hot((iota((slots_g, n), 0) + g * slots_g).astype(F32) == slot_r)
        rows = dot(pick, emb[...]).reshape(src_g, cap, W)
        xs[g * src_g : (g + 1) * src_g] = jnp.concatenate(
            [rows[:, :, w : w + LANES] for w in range(0, W, LANES)], axis=1
        ).astype(BF16)
    to_owner = hot(iota((R, n), 0).astype(F32) == rel_r)
    lane = iota((n, cap * sub), 1)
    slot_of_lane, field = (lane // sub).astype(F32), lane & (sub - 1)
    hi = jnp.floor(loc_c * (1.0 / 256.0))
    ids = jnp.where(field == 0, cid_c + 1.0, jnp.where(field == 1, loc_c - hi * 256.0, jnp.where(field == 2, hi + 1.0, 0.0)))
    mine = slot_of_lane == rank_c
    code_words = dot(to_owner, jnp.where(mine, pq_wide, 0.0).astype(BF16))
    id_words = dot(to_owner, jnp.where(mine, ids, 0.0).astype(BF16))
    ms[...] = jnp.concatenate([code_words, id_words], axis=1).reshape(R, 1, 2 * cap * sub)
    xr[0] = xs[0]
    mr[0] = ms[0]

    pl.semaphore_wait(gate, R - 1 + X - 1)

    def ar_core(inp, core, sems):
        remote(inp.at[1 - c], core, sems.at[0], at(dc=1), sems.at[8]).start()

    def ar_scatter(inp, core, rs, sems):
        arrived(core, sems.at[0])
        core[...] = core[...] + inp[c]
        for i in range(1, Y):
            remote(core.at[lax.rem(y + i, Y)], rs.at[0, i - 1], sems.at[1], at(dy=i), sems.at[9]).start()
        for i in range(1, Z):
            remote(core.at[Y + lax.rem(z + i, Z)], rs.at[1, i - 1], sems.at[2], at(dz=i), sems.at[10]).start()

    def ar_cross(core, rs, xx, sems):
        arrived(rs.at[0], sems.at[1])
        own_a = core[y] + jnp.sum(rs[0], axis=0)
        xx[0, z] = own_a
        for i in range(1, Z):
            remote(xx.at[0, z], xx.at[0, z], sems.at[3], at(dz=i), sems.at[11]).start()
        arrived(rs.at[1], sems.at[2])
        own_b = core[Y + z] + jnp.sum(rs[1], axis=0)
        xx[1, y] = own_b
        for i in range(1, Y):
            remote(xx.at[1, y], xx.at[1, y], sems.at[4], at(dy=i), sems.at[12]).start()

    def ar_gather(xx, full, sems, finish):
        arrived(rs_like(xx, Z), sems.at[3])
        full[c, y] = finish(jnp.sum(xx[0], axis=0), y)
        for i in range(1, Y):
            remote(full.at[c, y], full.at[c, y], sems.at[5], at(dy=i), sems.at[13]).start()
        arrived(rs_like(xx, Y), sems.at[4])
        full[c, Y + z] = finish(jnp.sum(xx[1], axis=0), Y + z)
        for i in range(1, Z):
            remote(full.at[c, Y + z], full.at[c, Y + z], sems.at[6], at(dz=i), sems.at[14]).start()

    def rs_like(xx, count):
        return xx.at[0, 0 : count - 1]

    def ar_pair(full, sems):
        arrived(full.at[0, 0 : Y - 1], sems.at[5])
        arrived(full.at[0, 0 : Z - 1], sems.at[6])
        remote(full.at[c], full.at[c], sems.at[7], at(dc=1), sems.at[15]).start()

    def ar_done(full, sems):
        arrived(full.at[0], sems.at[7])

    def ar_sent(inp, core, rs, xx, full, sems):
        arrived(core, sems.at[8])
        arrived(rs.at[0], sems.at[9])
        arrived(rs.at[1], sems.at[10])
        arrived(rs_like(xx, Z), sems.at[11])
        arrived(rs_like(xx, Y), sems.at[12])
        arrived(full.at[0, 0 : Y - 1], sems.at[13])
        arrived(full.at[0, 0 : Z - 1], sems.at[14])
        arrived(full.at[0], sems.at[15])

    def ship(g):
        def step(i, _):
            d = back(i)
            remote(xs.at[d], xr.at[i], s_x.at[g], offset_back(i), s_send.at[1]).start()
            return 0

        lax.fori_loop(max(1, g * src_g), (g + 1) * src_g, step, 0)

    def offset_back(i):
        return offset(back(i))

    def ship_words():
        def step(i, _):
            d = back(i)
            remote(ms.at[d], mr.at[i], s_m.at[0], offset_back(i), s_send.at[2]).start()
            return 0

        lax.fori_loop(1, R, step, 0)

    ar_core(in1, core1, s_ar1)
    ship(0)
    ar_scatter(in1, core1, rs1, s_ar1)
    ship_words()
    ar_cross(core1, rs1, x1, s_ar1)
    for g in range(1, groups // 2):
        ship(g)

    def coarse_mean(total, tile):
        first = pl.multiple_of(c * half + tile * TR, TR)
        count = total[:, W + sub : W + sub + 1]
        old = old_coarse[pl.ds(first, TR), :]
        mean = jnp.where(count > 0, total[:, :W] / jnp.maximum(count, 1.0), old)
        return jnp.concatenate([mean, total[:, W:]], axis=1)

    ar_gather(x1, full1, s_ar1, coarse_mean)
    for g in range(groups // 2, groups - 1):
        ship(g)
    ar_pair(full1, s_ar1)
    ship(groups - 1)

    def span(g):
        return slice(max(1, g * src_g), (g + 1) * src_g)

    arrived(mr.at[1:R], s_m.at[0])
    words = mr[...].reshape(R, 2 * cap * sub)
    code_w, id_w = words[:, : cap * sub], words[:, cap * sub :]
    by_src = hot((iota((S, R), 0) // cap) == iota((S, R), 1))
    mask_c = (iota((S, cap * sub), 1) // sub) == (iota((S, cap * sub), 0) & (cap - 1))
    pick_c = hot((iota((cap * sub, LANES), 0) & (sub - 1)) == iota((cap * sub, LANES), 1))
    id_c = dot(jnp.where(mask_c, dot(by_src, id_w.astype(BF16)), 0.0).astype(BF16), pick_c)
    by_src_t = hot((iota((R, S), 1) // cap) == iota((R, S), 0))
    mask_r = (iota((cap * sub, S), 0) // sub) == (iota((cap * sub, S), 1) & (cap - 1))
    pick_r = hot((iota((sub, cap * sub), 1) & (sub - 1)) == iota((sub, cap * sub), 0))

    def along_lanes(w):
        wide = dot(jnp.transpose(w).astype(BF16), by_src_t)
        return dot(pick_r, jnp.where(mask_r, wide, 0.0).astype(BF16))

    id_r, code_r = along_lanes(id_w), along_lanes(code_w)
    cid_slot = id_c[:, 0:1] - 1.0
    fid_slot = (id_c[:, 2:3] - 1.0) * 256.0 + id_c[:, 1:2]
    fid_lane = (id_r[2:3, :] - 1.0) * 256.0 + id_r[1:2, :]

    ar_done(full1, s_ar1)
    table = full1[...].reshape(K, W + LANES)
    o_coarse[...] = table[:, :W]
    coarse_parts = parts(table[:, :W], 3)

    fine_sum = jnp.zeros((fine_dev, W), F32)
    fine_count = jnp.zeros((fine_dev, 1), F32)
    for g in range(groups):
        arrived(xr.at[span(g)], s_x.at[g])
        lo = g * slots_g
        got = xr[g * src_g : (g + 1) * src_g].astype(F32)
        got = jnp.concatenate(
            [got[:, w * cap : (w + 1) * cap].reshape(slots_g, LANES) for w in range(W // LANES)], axis=1
        )
        c_hot = hot(iota((slots_g, K), 1).astype(F32) == cid_slot[lo : lo + slots_g])
        base = sum(dot(c_hot, p) for p in coarse_parts)
        cr = (got - base).astype(BF16)
        f_hot = iota((fine_dev, slots_g), 0).astype(F32) == fid_lane[:, lo : lo + slots_g]
        fine_sum += dot(hot(f_hot), cr)
        fine_count += jnp.sum(jnp.where(f_hot, 1.0, 0.0), axis=1, keepdims=True)
        cr_rows = cr.astype(F32).reshape(src_g, cap, W)
        xr[g * src_g : (g + 1) * src_g] = jnp.concatenate(
            [cr_rows[:, :, w : w + LANES] for w in range(0, W, LANES)], axis=1
        ).astype(BF16)
    new_fine = jnp.where(fine_count > 0, fine_sum / jnp.maximum(fine_count, 1.0), old_fine[...])
    o_fine[...] = new_fine
    fine_parts = parts(new_fine, 2)

    col = iota((1, W), 1) // sw
    code_sum = jnp.zeros((K, W), F32)
    for g in range(groups):
        lo = g * slots_g
        cr = xr[g * src_g : (g + 1) * src_g].astype(F32)
        cr = jnp.concatenate(
            [cr[:, w * cap : (w + 1) * cap].reshape(slots_g, LANES) for w in range(W // LANES)], axis=1
        )
        f_hot = hot(iota((slots_g, fine_dev), 1).astype(F32) == fid_slot[lo : lo + slots_g])
        res = (cr - sum(dot(f_hot, p) for p in fine_parts)).astype(BF16)
        res32 = res.astype(F32)
        res_rows = res32.reshape(src_g, cap, W)
        bs[g * src_g : (g + 1) * src_g] = jnp.concatenate(
            [res_rows[:, :, w : w + LANES] for w in range(0, W, LANES)], axis=1
        ).astype(BF16)

        def give(i, _):
            remote(bs.at[i], br.at[back(i)], s_b.at[0], offset(i), s_send.at[3]).start()
            return 0

        lax.fori_loop(max(1, g * src_g), (g + 1) * src_g, give, 0)
        for m in range(sub):
            k_hot = hot(iota((K, slots_g), 0).astype(F32) == code_r[m : m + 1, lo : lo + slots_g])
            code_sum += jnp.where(col == m, dot(k_hot, res), 0.0)
    in2[...] = code_sum.reshape(2, Y + Z, TR, W)
    br[0] = bs[0]

    counts = table[:, W:]
    widen = hot(iota((LANES, W), 1) // sw == iota((LANES, W), 0))
    count_wide = sum(dot(p, widen) for p in parts(counts, 2))

    ar_core(in2, core2, s_ar2)
    ar_scatter(in2, core2, rs2, s_ar2)
    ar_cross(core2, rs2, x2, s_ar2)
    ar_gather(x2, full2, s_ar2, lambda total, tile: total)
    ar_pair(full2, s_ar2)

    arrived(br.at[1:R], s_b.at[0])
    rows = br[...].astype(F32)
    rows = jnp.concatenate([rows[:, w * cap : (w + 1) * cap].reshape(S, LANES) for w in range(W // LANES)], axis=1)
    fetch = hot(iota((n, S), 1).astype(F32) == slot_c)
    res = dot(fetch, rows.astype(BF16))
    o_res[...] = res.astype(BF16)

    ar_done(full2, s_ar2)
    book = full2[...].reshape(K, W) / jnp.maximum(count_wide, 1.0)
    share = K // R
    me = (y * Z + z) * C + c
    tall = max(8, share)
    take = hot(iota((tall, K), 1) == iota((tall, K), 0) + me * share)
    own_book = sum(dot(take, p) for p in parts(book, 3))
    own_count = sum(dot(take, p) for p in parts(count_wide, 2))
    o_book[...] = jnp.where(own_count[:share] > 0, own_book[:share], old_book[...])
    book_parts = parts(book, 2)
    rebuilt = jnp.zeros((n, W), F32)
    for m in range(sub):
        k_hot = hot(iota((n, K), 1).astype(F32) == pq16[:, m : m + 1].astype(F32))
        rebuilt = jnp.where(col == m, sum(dot(k_hot, p) for p in book_parts), rebuilt)
    differ = res - rebuilt
    error = jnp.sum(differ * differ, axis=1, keepdims=True)
    error_row = jnp.sum(jnp.where(same, error, 0.0), axis=0, keepdims=True)
    err[x] = jnp.broadcast_to(error_row, (8, n))
    for d in range(1, X):
        remote(err.at[x], err.at[x], s_e.at[0], at(dx=d), s_send.at[4]).start()
    if X > 1:
        arrived(err.at[0 : X - 1], s_e.at[0])
    o_err[...] = jnp.sum(err[...], axis=0)[:1] * (1.0 / (W * X))

    if X > 1:
        arrived(err.at[0 : X - 1], s_send.at[4])
    arrived(xr.at[1:R], s_send.at[1])
    arrived(mr.at[1:R], s_send.at[2])
    arrived(br.at[1:R], s_send.at[3])
    ar_sent(in1, core1, rs1, x1, full1, s_ar1)
    ar_sent(in2, core2, rs2, x2, full2, s_ar2)


def shards(cfg, embeddings, coarse_ids, fine_ids, pq_codes, old_coarse, old_fine, old_codebook):
    n, W = embeddings.shape
    K, fine_dev, sub = old_coarse.shape[0], old_fine.shape[0], pq_codes.shape[1]
    Y, Z = cfg["Y"], cfg["Z"]
    R = Y * Z * cfg["C"]
    cap = 4 * n // R
    cfg = dict(cfg, R=R, n=n, W=W, cap=cap, fine_dev=fine_dev, K=K, sub=sub, groups=4)
    TR = K // 2 // (Y + Z)
    most = max(Y, Z)
    vm = pltpu.VMEM
    chunk = (R, cap * W // LANES, LANES)

    def ar(width):
        return [
            vm((2, Y + Z, TR, width), F32),
            vm((Y + Z, TR, width), F32),
            vm((2, most - 1, TR, width), F32),
            vm((2, most, TR, width), F32),
            vm((2, Y + Z, TR, width), F32),
        ]

    dma = pltpu.SemaphoreType.DMA
    outs = pl.pallas_call(
        functools.partial(kernel, cfg),
        out_shape=(
            jax.ShapeDtypeStruct((K, W), F32),
            jax.ShapeDtypeStruct((fine_dev, W), F32),
            jax.ShapeDtypeStruct((n, W), BF16),
            jax.ShapeDtypeStruct((K // R, W), F32),
            jax.ShapeDtypeStruct((1, n), F32),
        ),
        in_specs=[pl.BlockSpec(memory_space=vm)] * 7,
        out_specs=[pl.BlockSpec(memory_space=vm)] * 5,
        scratch_shapes=[
            vm(chunk, BF16),
            vm(chunk, BF16),
            vm((R, 1, 2 * cap * sub), F32),
            vm((R, 1, 2 * cap * sub), F32),
            vm(chunk, BF16),
            vm(chunk, BF16),
            *ar(W + LANES),
            *ar(W),
            vm((cfg["X"], 8, n), F32),
            dma((5,)),
            dma((4,)),
            dma((1,)),
            dma((1,)),
            dma((16,)),
            dma((16,)),
            dma((1,)),
        ],
        compiler_params=pltpu.CompilerParams(
            collective_id=0, has_side_effects=True, vmem_limit_bytes=48 * 2**20
        ),
    )(
        embeddings,
        coarse_ids.reshape(1, n),
        fine_ids.reshape(1, n),
        pq_codes,
        old_coarse,
        old_fine,
        old_codebook,
    )
    return (*outs[:4], outs[4].reshape(n))


def solution(mesh):
    devices = mesh.devices
    x = mesh.shape["rep"]
    chips = mesh.shape["rows"] // 2
    y = int(round(chips**0.5))
    z = chips // y
    torus = Mesh(devices.reshape(y, z, 2, x), (*ROWS, "rep"))
    cfg = {"Y": y, "Z": z, "C": 2, "X": x}
    return jax.shard_map(
        functools.partial(shards, cfg),
        mesh=torus,
        in_specs=(
            P(ROWS, "rep"),
            P(ROWS),
            P(ROWS),
            P(ROWS, "rep"),
            P(None, "rep"),
            P(ROWS, "rep"),
            P(ROWS, "rep"),
        ),
        out_specs=(P(None, "rep"), P(ROWS, "rep"), P(ROWS, "rep"), P(ROWS, "rep"), P(ROWS)),
        check_vma=False,
    )
```

```python
import functools

import jax
import jax.numpy as jnp
from jax import lax
from jax.experimental import pallas as pl
from jax.experimental.pallas import tpu as pltpu
from jax.sharding import Mesh
from jax.sharding import PartitionSpec as P

MESH = pl.DeviceIdType.MESH
ROWS = ("ry", "rz", "rc")
F32, BF16, I32 = jnp.float32, jnp.bfloat16, jnp.int32
LANES = 128


def iota(shape, dim):
    return lax.broadcasted_iota(I32, shape, dim)


def hot(cond):
    return jnp.where(cond, 1.0, 0.0).astype(BF16)


def dot(a, b):
    return jnp.dot(a, b, preferred_element_type=F32)


def parts(a, count):
    out = []
    for _ in range(count):
        p = a.astype(BF16)
        out.append(p)
        a = a - p.astype(F32)
    return out


def kernel(cfg, emb, cids, fids, pq_t, old_coarse, old_fine, old_book,
           o_coarse, o_fine, o_res, o_book, o_err,
           xs, xr, ms, mr, bs, br,
           in1, rs1, x1, full1,
           in2, rs2, x2, full2,
           err, held, coarse_old, fine_old, s_x, s_send, s_m, s_b, s_ar1, s_ar2, s_e, s_own):
    Y, Z, C, X = cfg["Y"], cfg["Z"], cfg["C"], cfg["X"]
    R, n, W, cap, fine_dev, K, sub = (cfg[k] for k in ("R", "n", "W", "cap", "fine_dev", "K", "sub"))
    S, half, TR, sw = R * cap, K // 2, K // 2 // (Y * C), W // sub
    groups = cfg["groups"]
    src_g, slots_g = R // groups, S // groups
    y, z, c, x = (lax.axis_index(a) for a in (*ROWS, "rep"))

    def at(dy=0, dz=0, dc=0, dx=0):
        return {
            "ry": (y + dy) & (Y - 1),
            "rz": (z + dz) & (Z - 1),
            "rc": (c + dc) & (C - 1),
            "rep": (x + dx) & (X - 1),
        }

    def peers(first, last, visit):
        def line(dy, skip=False):
            for dz in range(Z):
                for dc in range(C):
                    if not (skip and dz == 0 and dc == 0):
                        there = (dy * Z + dz) * C + dc
                        back = (((Y - dy) & (Y - 1)) * Z + (Z - dz) % Z) * C + (C - dc) % C
                        visit((dy, dz, dc), there, back)

        if first == 0:
            line(0, True)
            first = 1

        def step(dy, _):
            line(dy)
            return 0

        if last > first:
            lax.fori_loop(first, last, step, 0)

    def remote(src, dst, recv, where, send):
        return pltpu.make_async_remote_copy(src, dst, send, recv, device_id=where, device_id_type=MESH)

    def arrived(ref, sem):
        pltpu.make_async_copy(ref, ref, sem).wait()

    gate = pltpu.get_barrier_semaphore()

    def greet(off, there, back):
        pl.semaphore_signal(gate, inc=1, device_id=at(*off), device_id_type=MESH)

    peers(0, Y, greet)
    for d in range(1, X):
        pl.semaphore_signal(gate, inc=1, device_id=at(dx=d), device_id_type=MESH)

    tile_a, tile_b = y * C + c, z * C + c
    rows_a = pl.multiple_of(tile_a * TR, TR)
    rows_b = pl.multiple_of(half + tile_b * TR, TR)
    fetches = [
        pltpu.make_async_copy(old_coarse.at[pl.ds(rows_a, TR)], coarse_old.at[0], s_own.at[0]),
        pltpu.make_async_copy(old_coarse.at[pl.ds(rows_b, TR)], coarse_old.at[1], s_own.at[1]),
        pltpu.make_async_copy(old_fine, fine_old, s_own.at[2]),
    ]
    for f in fetches:
        f.start()

    cid_r, fid_r = cids[...], fids[...]
    own = fid_r // fine_dev
    loc = fid_r - own * fine_dev
    coarse_hot = hot(iota((K, n), 0) == cid_r)
    ones_lane = lambda lane: hot(iota((n, LANES), 1) == lane)
    pq_rows = pq_t[...].astype(F32)
    pq_tall = jnp.concatenate([pq_rows] * (LANES // sub), axis=0)
    pq16 = jnp.transpose(pq_tall)[:, :sub].astype(BF16)
    spread = hot((iota((sub, cap * sub), 1) & (sub - 1)) == iota((sub, cap * sub), 0))
    pq_wide = dot(pq16, spread)
    in1[:, :, :, :W] = dot(coarse_hot, emb[...]).reshape(2, Y * C, TR, W)
    tally = dot(coarse_hot, ones_lane(sub))
    for m in range(sub):
        tally += dot(hot(iota((K, n), 0).astype(F32) == pq_rows[m : m + 1, :]), ones_lane(m))
    in1[:, :, :, W:] = tally.reshape(2, Y * C, TR, LANES)

    rel_r = (
        ((own // (Z * C) - y) & (Y - 1)) * (Z * C) + (((own // C) - z) & (Z - 1)) * C + ((own - c) & (C - 1))
    ).astype(F32)
    same = iota((n, n), 0) == iota((n, n), 1)

    def column(row):
        return jnp.sum(jnp.where(same, row, 0.0), axis=1, keepdims=True)

    rel_c, cid_c, loc_c = column(rel_r), column(cid_r.astype(F32)), column(loc.astype(F32))
    eq = rel_c == rel_r
    before = iota((n, n), 0) < iota((n, n), 1)
    after = iota((n, n), 0) > iota((n, n), 1)
    rank_r = jnp.sum(jnp.where(eq & before, 1.0, 0.0), axis=0, keepdims=True)
    rank_c = jnp.sum(jnp.where(eq & after, 1.0, 0.0), axis=1, keepdims=True)
    slot_r = rel_r * cap + rank_r
    slot_c = rel_c * cap + rank_c
    for g in range(groups):
        pick = hot((iota((slots_g, n), 0) + g * slots_g).astype(F32) == slot_r)
        rows = dot(pick, emb[...]).reshape(src_g, cap, W)
        xs[g * src_g : (g + 1) * src_g] = jnp.concatenate(
            [rows[:, :, w : w + LANES] for w in range(0, W, LANES)], axis=1
        ).astype(BF16)
    to_owner = hot(iota((R, n), 0).astype(F32) == rel_r)
    lane = iota((n, cap * sub), 1)
    slot_of_lane, field = (lane // sub).astype(F32), lane & (sub - 1)
    hi = jnp.floor(loc_c * (1.0 / 256.0))
    ids = jnp.where(field == 0, cid_c + 1.0, jnp.where(field == 1, loc_c - hi * 256.0, jnp.where(field == 2, hi + 1.0, 0.0)))
    mine = slot_of_lane == rank_c
    code_words = dot(to_owner, jnp.where(mine, pq_wide, 0.0).astype(BF16))
    id_words = dot(to_owner, jnp.where(mine, ids, 0.0).astype(BF16))
    ms[...] = jnp.concatenate([code_words, id_words], axis=1).reshape(R, 1, 2 * cap * sub)
    xr[0] = xs[0]
    mr[0] = ms[0]

    pl.semaphore_wait(gate, R - 1 + X - 1)

    def line_peers(along):
        for i in range(1, (Z if along else Y) * C):
            d, dc = i // C, i % C
            yield i, ((at(dz=d, dc=dc), ((z + d) & (Z - 1)) * C + ((c + dc) & (C - 1))) if along else
                      (at(dy=d, dc=dc), ((y + d) & (Y - 1)) * C + ((c + dc) & (C - 1))))

    def ar_scatter(inp, rs, sems):
        for along in range(2):
            for i, (where, tile) in line_peers(along):
                remote(inp.at[along, tile], rs.at[along, i - 1], sems.at[along], where, sems.at[6 + along]).start()

    def ar_cross(inp, rs, xx, sems):
        for along, tile, place, count in ((0, tile_a, z, Z), (1, tile_b, y, Y)):
            arrived(rs.at[along], sems.at[along])
            xx[along, place] = inp[along, tile] + jnp.sum(rs[along], axis=0)
            for i in range(1, count):
                where = at(dy=i) if along else at(dz=i)
                remote(
                    xx.at[along, place], xx.at[along, place], sems.at[2 + along], where, sems.at[8 + along]
                ).start()

    def others(ref, along):
        return ref.at[along, 0 : (Y if along else Z) - 1]

    def line_of(full, along):
        return full.at[along, 0 : (Z if along else Y) * C - 1]

    def ar_gather(xx, full, sems, finish):
        for along, tile in ((0, tile_a), (1, tile_b)):
            arrived(others(xx, along), sems.at[2 + along])
            full[along, tile] = finish(jnp.sum(xx[along], axis=0), along)
            for i, (where, _) in line_peers(along):
                remote(
                    full.at[along, tile], full.at[along, tile], sems.at[4 + along], where, sems.at[10 + along]
                ).start()

    def ar_done(full, sems):
        for along in range(2):
            arrived(line_of(full, along), sems.at[4 + along])

    def ar_sent(rs, xx, full, sems):
        for along in range(2):
            arrived(rs.at[along], sems.at[6 + along])
            arrived(others(xx, along), sems.at[8 + along])
            arrived(line_of(full, along), sems.at[10 + along])

    per_group = Y // groups

    def ship(g):
        def visit(off, i, d):
            remote(xs.at[d], xr.at[i], s_x.at[g], at(-off[0], -off[1], -off[2]), s_send.at[0]).start()

        peers(g * per_group, (g + 1) * per_group, visit)

    def ship_words():
        def visit(off, i, d):
            remote(ms.at[d], mr.at[i], s_m.at[0], at(-off[0], -off[1], -off[2]), s_send.at[1]).start()

        peers(0, Y, visit)

    def give(g):
        def visit(off, i, d):
            remote(bs.at[i], br.at[d], s_b.at[0], at(*off), s_send.at[2]).start()

        peers(g * per_group, (g + 1) * per_group, visit)

    ar_scatter(in1, rs1, s_ar1)
    ship(0)
    ar_cross(in1, rs1, x1, s_ar1)
    ship(1)

    def coarse_mean(total, along):
        fetches[along].wait()
        count = total[:, W + sub : W + sub + 1]
        held[along] = total[:, W:]
        return jnp.where(count > 0, total[:, :W] / jnp.maximum(count, 1.0), coarse_old[along])

    ar_gather(x1, full1, s_ar1, coarse_mean)
    ship_words()
    for g in range(2, groups):
        ship(g)

    def span(g):
        return slice(max(1, g * src_g), (g + 1) * src_g)

    arrived(mr.at[1:R], s_m.at[0])
    words = mr[...].reshape(R, 2 * cap * sub)
    code_w, id_w = words[:, : cap * sub], words[:, cap * sub :]
    by_src = hot((iota((S, R), 0) // cap) == iota((S, R), 1))
    mask_c = (iota((S, cap * sub), 1) // sub) == (iota((S, cap * sub), 0) & (cap - 1))
    pick_c = hot((iota((cap * sub, LANES), 0) & (sub - 1)) == iota((cap * sub, LANES), 1))
    id_c = dot(jnp.where(mask_c, dot(by_src, id_w.astype(BF16)), 0.0).astype(BF16), pick_c)
    by_src_t = hot((iota((R, S), 1) // cap) == iota((R, S), 0))
    mask_r = (iota((cap * sub, S), 0) // sub) == (iota((cap * sub, S), 1) & (cap - 1))
    pick_r = hot((iota((sub, cap * sub), 1) & (sub - 1)) == iota((sub, cap * sub), 0))

    def along_lanes(w):
        wide = dot(jnp.transpose(w).astype(BF16), by_src_t)
        return dot(pick_r, jnp.where(mask_r, wide, 0.0).astype(BF16))

    id_r, code_r = along_lanes(id_w), along_lanes(code_w)
    cid_slot = id_c[:, 0:1] - 1.0
    fid_slot = (id_c[:, 2:3] - 1.0) * 256.0 + id_c[:, 1:2]
    fid_lane = (id_r[2:3, :] - 1.0) * 256.0 + id_r[1:2, :]

    ar_done(full1, s_ar1)
    table = full1[...].reshape(K, W)
    o_coarse[...] = table
    coarse_parts = parts(table, 3)

    fine_sum = jnp.zeros((fine_dev, W), F32)
    fine_count = jnp.zeros((fine_dev, 1), F32)
    for g in range(groups):
        arrived(xr.at[span(g)], s_x.at[g])
        lo = g * slots_g
        got = xr[g * src_g : (g + 1) * src_g].astype(F32)
        got = jnp.concatenate(
            [got[:, w * cap : (w + 1) * cap].reshape(slots_g, LANES) for w in range(W // LANES)], axis=1
        )
        c_hot = hot(iota((slots_g, K), 1).astype(F32) == cid_slot[lo : lo + slots_g])
        base = sum(dot(c_hot, p) for p in coarse_parts)
        cr = (got - base).astype(BF16)
        f_hot = iota((fine_dev, slots_g), 0).astype(F32) == fid_lane[:, lo : lo + slots_g]
        fine_sum += dot(hot(f_hot), cr)
        fine_count += jnp.sum(jnp.where(f_hot, 1.0, 0.0), axis=1, keepdims=True)
        cr_rows = cr.astype(F32).reshape(src_g, cap, W)
        xr[g * src_g : (g + 1) * src_g] = jnp.concatenate(
            [cr_rows[:, :, w : w + LANES] for w in range(0, W, LANES)], axis=1
        ).astype(BF16)
    fetches[2].wait()
    new_fine = jnp.where(fine_count > 0, fine_sum / jnp.maximum(fine_count, 1.0), fine_old[...])
    o_fine[...] = new_fine
    fine_parts = parts(new_fine, 2)

    col = iota((1, W), 1) // sw
    code_sum = jnp.zeros((K, W), F32)
    for g in range(groups):
        lo = g * slots_g
        cr = xr[g * src_g : (g + 1) * src_g].astype(F32)
        cr = jnp.concatenate(
            [cr[:, w * cap : (w + 1) * cap].reshape(slots_g, LANES) for w in range(W // LANES)], axis=1
        )
        f_hot = hot(iota((slots_g, fine_dev), 1).astype(F32) == fid_slot[lo : lo + slots_g])
        res = (cr - sum(dot(f_hot, p) for p in fine_parts)).astype(BF16)
        res32 = res.astype(F32)
        res_rows = res32.reshape(src_g, cap, W)
        bs[g * src_g : (g + 1) * src_g] = jnp.concatenate(
            [res_rows[:, :, w : w + LANES] for w in range(0, W, LANES)], axis=1
        ).astype(BF16)

        for m in range(sub):
            k_hot = hot(iota((K, slots_g), 0).astype(F32) == code_r[m : m + 1, lo : lo + slots_g])
            code_sum += jnp.where(col == m, dot(k_hot, res), 0.0)
    in2[...] = code_sum.reshape(2, Y * C, TR, W)
    br[0] = bs[0]

    widen = hot(iota((LANES, W), 1) // sw == iota((LANES, W), 0))
    none = 1e30

    def code_mean(total, along):
        count = sum(dot(p, widen) for p in parts(held[along], 2))
        return jnp.where(count > 0, total / jnp.maximum(count, 1.0), none)

    ar_scatter(in2, rs2, s_ar2)
    give(0)
    ar_cross(in2, rs2, x2, s_ar2)
    give(1)
    ar_gather(x2, full2, s_ar2, code_mean)
    for g in range(2, groups):
        give(g)

    arrived(br.at[1:R], s_b.at[0])
    rows = br[...].astype(F32)
    rows = jnp.concatenate([rows[:, w * cap : (w + 1) * cap].reshape(S, LANES) for w in range(W // LANES)], axis=1)
    fetch = hot(iota((n, S), 1).astype(F32) == slot_c)
    res = dot(fetch, rows.astype(BF16))
    o_res[...] = res.astype(BF16)

    ar_done(full2, s_ar2)
    book = full2[...].reshape(K, W)
    share = K // R
    me = (y * Z + z) * C + c
    tall = max(8, share)
    take = hot(iota((tall, K), 1) == iota((tall, K), 0) + me * share)
    own_book = sum(dot(take, p) for p in parts(book, 3))
    o_book[...] = jnp.where(own_book[:share] < 0.5 * none, own_book[:share], old_book[...])
    book_parts = parts(book, 2)
    rebuilt = jnp.zeros((n, W), F32)
    for m in range(sub):
        k_hot = hot(iota((n, K), 1).astype(F32) == pq16[:, m : m + 1].astype(F32))
        rebuilt = jnp.where(col == m, sum(dot(k_hot, p) for p in book_parts), rebuilt)
    differ = res - rebuilt
    error = jnp.sum(differ * differ, axis=1, keepdims=True)
    error_row = jnp.sum(jnp.where(same, error, 0.0), axis=0, keepdims=True)
    err[x] = jnp.broadcast_to(error_row, (8, n))
    for d in range(1, X):
        remote(err.at[x], err.at[x], s_e.at[0], at(dx=d), s_send.at[3]).start()
    if X > 1:
        arrived(err.at[0 : X - 1], s_e.at[0])
    o_err[...] = (jnp.sum(err[...], axis=0)[:1] * (1.0 / (W * X))).reshape(n)

    if X > 1:
        arrived(err.at[0 : X - 1], s_send.at[3])
    arrived(xr.at[1:R], s_send.at[0])
    arrived(mr.at[1:R], s_send.at[1])
    arrived(br.at[1:R], s_send.at[2])
    ar_sent(rs1, x1, full1, s_ar1)
    ar_sent(rs2, x2, full2, s_ar2)


def hand_over(*refs):
    count = (len(refs) - 1) // 2
    copies = [pltpu.make_async_copy(refs[i], refs[count + i], refs[-1].at[i]) for i in range(count)]
    for f in copies:
        f.start()
    for f in copies:
        f.wait()


def shards(cfg, embeddings, coarse_ids, fine_ids, pq_codes, old_coarse, old_fine, old_codebook):
    n, W = embeddings.shape
    K, fine_dev, sub = old_coarse.shape[0], old_fine.shape[0], pq_codes.shape[1]
    Y, Z = cfg["Y"], cfg["Z"]
    R = Y * Z * cfg["C"]
    cap = 4 * n // R
    cfg = dict(cfg, R=R, n=n, W=W, cap=cap, fine_dev=fine_dev, K=K, sub=sub, groups=min(4, Y))
    tiles = Y * cfg["C"]
    TR = K // 2 // tiles
    most = max(Y, Z)
    vm = pltpu.VMEM
    chunk = (R, cap * W // LANES, LANES)

    def ar(width):
        return [
            vm((2, tiles, TR, width), F32),
            vm((2, tiles - 1, TR, width), F32),
            vm((2, most, TR, width), F32),
            vm((2, tiles, TR, W), F32),
        ]

    dma = pltpu.SemaphoreType.DMA
    outs = pl.pallas_call(
        functools.partial(kernel, cfg),
        out_shape=(
            jax.ShapeDtypeStruct((K, W), F32),
            jax.ShapeDtypeStruct((fine_dev, W), F32),
            jax.ShapeDtypeStruct((n, W), BF16),
            jax.ShapeDtypeStruct((K // R, W), F32),
            jax.ShapeDtypeStruct((n,), F32),
        ),
        in_specs=[pl.BlockSpec(memory_space=vm)] * 4 + [pl.BlockSpec(memory_space=pl.ANY)] * 2 + [pl.BlockSpec(memory_space=vm)],
        out_specs=[pl.BlockSpec(memory_space=vm)] * 5,
        scratch_shapes=[
            vm(chunk, BF16),
            vm(chunk, BF16),
            vm((R, 1, 2 * cap * sub), F32),
            vm((R, 1, 2 * cap * sub), F32),
            vm(chunk, BF16),
            vm(chunk, BF16),
            *ar(W + LANES),
            *ar(W),
            vm((cfg["X"], 8, n), F32),
            vm((2, TR, LANES), F32),
            vm((2, TR, W), F32),
            vm((fine_dev, W), F32),
            dma((4,)),
            dma((4,)),
            dma((1,)),
            dma((1,)),
            dma((12,)),
            dma((12,)),
            dma((1,)),
            dma((3,)),
        ],
        compiler_params=pltpu.CompilerParams(
            collective_id=0, has_side_effects=True, vmem_limit_bytes=56 * 2**20
        ),
    )(
        embeddings,
        coarse_ids.reshape(1, n),
        fine_ids.reshape(1, n),
        pq_codes.T,
        old_coarse,
        old_fine,
        old_codebook,
    )
    return pl.pallas_call(
        hand_over,
        out_shape=tuple(jax.ShapeDtypeStruct(o.shape, o.dtype) for o in outs),
        in_specs=[pl.BlockSpec(memory_space=pl.ANY)] * 5,
        out_specs=[pl.BlockSpec(memory_space=pl.ANY)] * 5,
        scratch_shapes=[dma((5,))],
    )(*outs)


def solution(mesh):
    devices = mesh.devices
    x = mesh.shape["rep"]
    chips = mesh.shape["rows"] // 2
    y = int(round(chips**0.5))
    z = chips // y
    torus = Mesh(devices.reshape(y, z, 2, x), (*ROWS, "rep"))
    cfg = {"Y": y, "Z": z, "C": 2, "X": x}
    return jax.shard_map(
        functools.partial(shards, cfg),
        mesh=torus,
        in_specs=(
            P(ROWS, "rep"),
            P(ROWS),
            P(ROWS),
            P(ROWS, "rep"),
            P(None, "rep"),
            P(ROWS, "rep"),
            P(ROWS, "rep"),
        ),
        out_specs=(P(None, "rep"), P(ROWS, "rep"), P(ROWS, "rep"), P(ROWS, "rep"), P(ROWS)),
        check_vma=False,
    )
```

```python
import functools

import jax
import jax.numpy as jnp
from jax import lax
from jax.experimental import pallas as pl
from jax.experimental.pallas import tpu as pltpu
from jax.sharding import Mesh
from jax.sharding import PartitionSpec as P

MESH = pl.DeviceIdType.MESH
ROWS = ("ry", "rz", "rc")
F32, BF16, I32 = jnp.float32, jnp.bfloat16, jnp.int32
LANES = 128


def iota(shape, dim):
    return lax.broadcasted_iota(I32, shape, dim)


def hot(cond):
    return jnp.where(cond, 1.0, 0.0).astype(BF16)


def dot(a, b):
    return jnp.dot(a, b, preferred_element_type=F32)


def parts(a, count):
    out = []
    for _ in range(count):
        p = a.astype(BF16)
        out.append(p)
        a = a - p.astype(F32)
    return out


def kernel(cfg, emb, cids, fids, pq, old_coarse, old_fine, old_book,
           o_coarse, o_fine, o_res, o_book, o_err,
           xs, xr, ms, mr, bs, br,
           in1, core1, rs1, x1, full1,
           in2, core2, rs2, x2, full2,
           err, coarse_old, fine_old, s_own, s_send, s_x, s_m, s_b, s_ar1, s_ar2, s_e):
    Y, Z, C, X = cfg["Y"], cfg["Z"], cfg["C"], cfg["X"]
    R, n, W, cap, fine_dev, K, sub = (cfg[k] for k in ("R", "n", "W", "cap", "fine_dev", "K", "sub"))
    S, half, TR, sw = R * cap, K // 2, K // 2 // (Y + Z), W // sub
    groups = cfg["groups"]
    src_g, slots_g = R // groups, S // groups
    y, z, c, x = (lax.axis_index(a) for a in (*ROWS, "rep"))

    def at(dy=0, dz=0, dc=0, dx=0):
        return {
            "ry": (y + dy) & (Y - 1),
            "rz": (z + dz) & (Z - 1),
            "rc": (c + dc) & (C - 1),
            "rep": (x + dx) & (X - 1),
        }

    zs = sorted(range(Z), key=lambda d: (min(d, Z - d), d))

    def pair(k, visit):
        first = isinstance(k, int) and k == 0
        for dz in zs:
            for dc in range(C):
                for side in range(2):
                    if first and side == dz == dc == 0:
                        continue
                    dy = (0, Y // 2)[side] if first else (k, Y - k)[side]
                    other = side if first else 1 - side
                    there = ((2 * k + side) * Z + dz) * C + dc
                    back = ((2 * k + other) * Z + (Z - dz) % Z) * C + (C - dc) % C
                    visit((dy, dz, dc), there, back)

    def peers(visit):
        pair(0, visit)

        def step(k, _):
            pair(k, visit)
            return 0

        if Y > 2:
            lax.fori_loop(1, Y // 2, step, 0)

    def remote(src, dst, recv, where, send):
        return pltpu.make_async_remote_copy(src, dst, send, recv, device_id=where, device_id_type=MESH)

    def arrived(ref, sem):
        pltpu.make_async_copy(ref, ref, sem).wait()

    gate = pltpu.get_barrier_semaphore()

    def greet(off, there, back):
        pl.semaphore_signal(gate, inc=1, device_id=at(*off), device_id_type=MESH)

    peers(greet)
    for d in range(1, X):
        pl.semaphore_signal(gate, inc=1, device_id=at(dx=d), device_id_type=MESH)

    fetches = [
        pltpu.make_async_copy(old_coarse, coarse_old, s_own.at[0]),
        pltpu.make_async_copy(old_fine, fine_old, s_own.at[1]),
    ]
    for f in fetches:
        f.start()

    cid_r, fid_r = cids[...], fids[...]
    own = fid_r // fine_dev
    loc = fid_r - own * fine_dev
    coarse_hot = hot(iota((K, n), 0) == cid_r)
    ones_lane = lambda lane: hot(iota((n, LANES), 1) == lane)
    pq_rows = pq[...].astype(F32)
    pq16 = jnp.transpose(jnp.concatenate([pq_rows] * (LANES // sub), axis=0))[:, :sub].astype(BF16)
    spread = hot((iota((sub, cap * sub), 1) & (sub - 1)) == iota((sub, cap * sub), 0))
    pq_wide = dot(pq16, spread)
    in1[:, :, :, :W] = dot(coarse_hot, emb[...]).reshape(2, Y + Z, TR, W)
    tally = dot(coarse_hot, ones_lane(sub))
    for m in range(sub):
        tally += dot(hot(iota((K, n), 0).astype(F32) == pq_rows[m : m + 1, :]), ones_lane(m))
    in1[:, :, :, W:] = tally.reshape(2, Y + Z, TR, LANES)

    turn = ((own // (Z * C)) - y) & (Y - 1)
    place_y = jnp.where(turn == 0, 0, jnp.where(turn == Y // 2, 1, jnp.where(turn < Y // 2, 2 * turn, 2 * (Y - turn) + 1)))
    rel_r = (
        place_y * (Z * C) + (((own // C) - z) & (Z - 1)) * C + ((own - c) & (C - 1))
    ).astype(F32)
    same = iota((n, n), 0) == iota((n, n), 1)

    def column(row):
        return jnp.sum(jnp.where(same, row, 0.0), axis=1, keepdims=True)

    rel_c, cid_c, loc_c = column(rel_r), column(cid_r.astype(F32)), column(loc.astype(F32))
    eq = rel_c == rel_r
    before = iota((n, n), 0) < iota((n, n), 1)
    after = iota((n, n), 0) > iota((n, n), 1)
    rank_r = jnp.sum(jnp.where(eq & before, 1.0, 0.0), axis=0, keepdims=True)
    rank_c = jnp.sum(jnp.where(eq & after, 1.0, 0.0), axis=1, keepdims=True)
    slot_r = rel_r * cap + rank_r
    slot_c = rel_c * cap + rank_c
    for g in range(groups):
        pick = hot((iota((slots_g, n), 0) + g * slots_g).astype(F32) == slot_r)
        rows = dot(pick, emb[...]).reshape(src_g, cap, W)
        xs[g * src_g : (g + 1) * src_g] = jnp.concatenate(
            [rows[:, :, w : w + LANES] for w in range(0, W, LANES)], axis=1
        ).astype(BF16)
    to_owner = hot(iota((R, n), 0).astype(F32) == rel_r)
    lane = iota((n, cap * sub), 1)
    slot_of_lane, field = (lane // sub).astype(F32), lane & (sub - 1)
    hi = jnp.floor(loc_c * (1.0 / 256.0))
    ids = jnp.where(field == 0, cid_c + 1.0, jnp.where(field == 1, loc_c - hi * 256.0, jnp.where(field == 2, hi + 1.0, 0.0)))
    mine = slot_of_lane == rank_c
    code_words = dot(to_owner, jnp.where(mine, pq_wide, 0.0).astype(BF16))
    id_words = dot(to_owner, jnp.where(mine, ids, 0.0).astype(BF16))
    ms[...] = jnp.concatenate([code_words, id_words], axis=1).reshape(R, 1, 2 * cap * sub)
    xr[0] = xs[0]
    mr[0] = ms[0]

    pl.semaphore_wait(gate, R - 1 + X - 1)

    def ar_core(inp, core, sems):
        remote(inp.at[1 - c], core, sems.at[0], at(dc=1), sems.at[8]).start()

    def ar_scatter(inp, core, rs, sems):
        arrived(core, sems.at[0])
        core[...] = core[...] + inp[c]
        for i in range(1, Y):
            remote(core.at[lax.rem(y + i, Y)], rs.at[0, i - 1], sems.at[1], at(dy=i), sems.at[9]).start()
        for i in range(1, Z):
            remote(core.at[Y + lax.rem(z + i, Z)], rs.at[1, i - 1], sems.at[2], at(dz=i), sems.at[10]).start()

    def ar_cross(core, rs, xx, sems):
        arrived(rs.at[0], sems.at[1])
        own_a = core[y] + jnp.sum(rs[0], axis=0)
        xx[0, z] = own_a
        for i in range(1, Z):
            remote(xx.at[0, z], xx.at[0, z], sems.at[3], at(dz=i), sems.at[11]).start()
        arrived(rs.at[1], sems.at[2])
        own_b = core[Y + z] + jnp.sum(rs[1], axis=0)
        xx[1, y] = own_b
        for i in range(1, Y):
            remote(xx.at[1, y], xx.at[1, y], sems.at[4], at(dy=i), sems.at[12]).start()

    def ar_gather(xx, full, sems, finish):
        arrived(rs_like(xx, Z), sems.at[3])
        full[c, y] = finish(jnp.sum(xx[0], axis=0), y)
        for i in range(1, Y):
            remote(full.at[c, y], full.at[c, y], sems.at[5], at(dy=i), sems.at[13]).start()
        arrived(rs_like(xx, Y), sems.at[4])
        full[c, Y + z] = finish(jnp.sum(xx[1], axis=0), Y + z)
        for i in range(1, Z):
            remote(full.at[c, Y + z], full.at[c, Y + z], sems.at[6], at(dz=i), sems.at[14]).start()

    def rs_like(xx, count):
        return xx.at[0, 0 : count - 1]

    def ar_pair(full, sems):
        arrived(full.at[0, 0 : Y - 1], sems.at[5])
        arrived(full.at[0, 0 : Z - 1], sems.at[6])
        remote(full.at[c], full.at[c], sems.at[7], at(dc=1), sems.at[15]).start()

    def ar_done(full, sems):
        arrived(full.at[0], sems.at[7])

    def ar_sent(inp, core, rs, xx, full, sems):
        arrived(core, sems.at[8])
        arrived(rs.at[0], sems.at[9])
        arrived(rs.at[1], sems.at[10])
        arrived(rs_like(xx, Z), sems.at[11])
        arrived(rs_like(xx, Y), sems.at[12])
        arrived(full.at[0, 0 : Y - 1], sems.at[13])
        arrived(full.at[0, 0 : Z - 1], sems.at[14])
        arrived(full.at[0], sems.at[15])

    def ship(g):
        def visit(off, i, d):
            remote(xs.at[d], xr.at[i], s_x.at[g], at(-off[0], -off[1], -off[2]), s_send.at[1]).start()

        pair(g, visit)

    def ship_words():
        def visit(off, i, d):
            remote(ms.at[d], mr.at[i], s_m.at[0], at(-off[0], -off[1], -off[2]), s_send.at[2]).start()

        peers(visit)

    def give(g):
        def visit(off, i, d):
            remote(bs.at[i], br.at[d], s_b.at[0], at(*off), s_send.at[3]).start()

        if g < groups:
            pair(g, visit)

    ar_core(in1, core1, s_ar1)
    ship(0)
    ar_scatter(in1, core1, rs1, s_ar1)
    ship_words()
    ar_cross(core1, rs1, x1, s_ar1)
    for g in range(1, groups // 2):
        ship(g)

    fetches[0].wait()

    def coarse_mean(total, tile):
        first = pl.multiple_of(c * half + tile * TR, TR)
        count = total[:, W + sub : W + sub + 1]
        old = coarse_old[pl.ds(first, TR), :]
        mean = jnp.where(count > 0, total[:, :W] / jnp.maximum(count, 1.0), old)
        return jnp.concatenate([mean, total[:, W:]], axis=1)

    ar_gather(x1, full1, s_ar1, coarse_mean)
    for g in range(groups // 2, groups - 1):
        ship(g)
    ar_pair(full1, s_ar1)
    if groups > 1:
        ship(groups - 1)

    def span(g):
        return slice(max(1, g * src_g), (g + 1) * src_g)

    arrived(mr.at[1:R], s_m.at[0])
    words = mr[...].reshape(R, 2 * cap * sub)
    code_w, id_w = words[:, : cap * sub], words[:, cap * sub :]
    by_src = hot((iota((S, R), 0) // cap) == iota((S, R), 1))
    mask_c = (iota((S, cap * sub), 1) // sub) == (iota((S, cap * sub), 0) & (cap - 1))
    pick_c = hot((iota((cap * sub, LANES), 0) & (sub - 1)) == iota((cap * sub, LANES), 1))
    id_c = dot(jnp.where(mask_c, dot(by_src, id_w.astype(BF16)), 0.0).astype(BF16), pick_c)
    by_src_t = hot((iota((R, S), 1) // cap) == iota((R, S), 0))
    mask_r = (iota((cap * sub, S), 0) // sub) == (iota((cap * sub, S), 1) & (cap - 1))
    pick_r = hot((iota((sub, cap * sub), 1) & (sub - 1)) == iota((sub, cap * sub), 0))

    def along_lanes(w):
        wide = dot(jnp.transpose(w).astype(BF16), by_src_t)
        return dot(pick_r, jnp.where(mask_r, wide, 0.0).astype(BF16))

    id_r, code_r = along_lanes(id_w), along_lanes(code_w)
    cid_slot = id_c[:, 0:1] - 1.0
    fid_slot = (id_c[:, 2:3] - 1.0) * 256.0 + id_c[:, 1:2]
    fid_lane = (id_r[2:3, :] - 1.0) * 256.0 + id_r[1:2, :]

    ar_done(full1, s_ar1)
    table = full1[...].reshape(K, W + LANES)
    o_coarse[...] = table[:, :W]
    coarse_parts = parts(table[:, :W], 3)

    fine_sum = jnp.zeros((fine_dev, W), F32)
    fine_count = jnp.zeros((fine_dev, 1), F32)
    for g in range(groups):
        arrived(xr.at[span(g)], s_x.at[g])
        lo = g * slots_g
        got = xr[g * src_g : (g + 1) * src_g].astype(F32)
        got = jnp.concatenate(
            [got[:, w * cap : (w + 1) * cap].reshape(slots_g, LANES) for w in range(W // LANES)], axis=1
        )
        c_hot = hot(iota((slots_g, K), 1).astype(F32) == cid_slot[lo : lo + slots_g])
        base = sum(dot(c_hot, p) for p in coarse_parts)
        cr = (got - base).astype(BF16)
        f_hot = iota((fine_dev, slots_g), 0).astype(F32) == fid_lane[:, lo : lo + slots_g]
        fine_sum += dot(hot(f_hot), cr)
        fine_count += jnp.sum(jnp.where(f_hot, 1.0, 0.0), axis=1, keepdims=True)
        cr_rows = cr.astype(F32).reshape(src_g, cap, W)
        xr[g * src_g : (g + 1) * src_g] = jnp.concatenate(
            [cr_rows[:, :, w : w + LANES] for w in range(0, W, LANES)], axis=1
        ).astype(BF16)
    fetches[1].wait()
    new_fine = jnp.where(fine_count > 0, fine_sum / jnp.maximum(fine_count, 1.0), fine_old[...])
    o_fine[...] = new_fine
    fine_parts = parts(new_fine, 2)

    col = iota((1, W), 1) // sw
    code_sum = jnp.zeros((K, W), F32)
    for g in range(groups):
        lo = g * slots_g
        cr = xr[g * src_g : (g + 1) * src_g].astype(F32)
        cr = jnp.concatenate(
            [cr[:, w * cap : (w + 1) * cap].reshape(slots_g, LANES) for w in range(W // LANES)], axis=1
        )
        f_hot = hot(iota((slots_g, fine_dev), 1).astype(F32) == fid_slot[lo : lo + slots_g])
        res = (cr - sum(dot(f_hot, p) for p in fine_parts)).astype(BF16)
        res32 = res.astype(F32)
        res_rows = res32.reshape(src_g, cap, W)
        bs[g * src_g : (g + 1) * src_g] = jnp.concatenate(
            [res_rows[:, :, w : w + LANES] for w in range(0, W, LANES)], axis=1
        ).astype(BF16)

        for m in range(sub):
            k_hot = hot(iota((K, slots_g), 0).astype(F32) == code_r[m : m + 1, lo : lo + slots_g])
            code_sum += jnp.where(col == m, dot(k_hot, res), 0.0)
    in2[...] = code_sum.reshape(2, Y + Z, TR, W)
    ar_core(in2, core2, s_ar2)
    br[0] = bs[0]

    counts = table[:, W:]
    widen = hot(iota((LANES, W), 1) // sw == iota((LANES, W), 0))
    count_wide = sum(dot(p, widen) for p in parts(counts, 2))

    give(0)
    ar_scatter(in2, core2, rs2, s_ar2)
    give(1)
    ar_cross(core2, rs2, x2, s_ar2)
    give(2)
    ar_gather(x2, full2, s_ar2, lambda total, tile: total)
    give(3)
    ar_pair(full2, s_ar2)

    arrived(br.at[1:R], s_b.at[0])
    rows = br[...].astype(F32)
    rows = jnp.concatenate([rows[:, w * cap : (w + 1) * cap].reshape(S, LANES) for w in range(W // LANES)], axis=1)
    fetch = hot(iota((n, S), 1).astype(F32) == slot_c)
    res = dot(fetch, rows.astype(BF16))
    o_res[...] = res.astype(BF16)

    ar_done(full2, s_ar2)
    book = full2[...].reshape(K, W) / jnp.maximum(count_wide, 1.0)
    share = K // R
    me = (y * Z + z) * C + c
    tall = max(8, share)
    take = hot(iota((tall, K), 1) == iota((tall, K), 0) + me * share)
    own_book = sum(dot(take, p) for p in parts(book, 3))
    own_count = sum(dot(take, p) for p in parts(count_wide, 2))
    o_book[...] = jnp.where(own_count[:share] > 0, own_book[:share], old_book[...])
    book_parts = parts(book, 2)
    rebuilt = jnp.zeros((n, W), F32)
    for m in range(sub):
        k_hot = hot(iota((n, K), 1).astype(F32) == pq16[:, m : m + 1].astype(F32))
        rebuilt = jnp.where(col == m, sum(dot(k_hot, p) for p in book_parts), rebuilt)
    differ = res - rebuilt
    error = jnp.sum(differ * differ, axis=1, keepdims=True)
    error_row = jnp.sum(jnp.where(same, error, 0.0), axis=0, keepdims=True)
    err[x] = jnp.broadcast_to(error_row, (8, n))
    for d in range(1, X):
        remote(err.at[x], err.at[x], s_e.at[0], at(dx=d), s_send.at[4]).start()
    if X > 1:
        arrived(err.at[0 : X - 1], s_e.at[0])
    o_err[...] = (jnp.sum(err[...], axis=0)[:1] * (1.0 / (W * X))).reshape(n)

    if X > 1:
        arrived(err.at[0 : X - 1], s_send.at[4])
    arrived(xr.at[1:R], s_send.at[1])
    arrived(mr.at[1:R], s_send.at[2])
    arrived(br.at[1:R], s_send.at[3])
    ar_sent(in1, core1, rs1, x1, full1, s_ar1)
    ar_sent(in2, core2, rs2, x2, full2, s_ar2)


def shards(cfg, embeddings, coarse_ids, fine_ids, pq_codes, old_coarse, old_fine, old_codebook):
    n, W = embeddings.shape
    K, fine_dev, sub = old_coarse.shape[0], old_fine.shape[0], pq_codes.shape[1]
    Y, Z = cfg["Y"], cfg["Z"]
    R = Y * Z * cfg["C"]
    cap = 4 * n // R
    cfg = dict(cfg, R=R, n=n, W=W, cap=cap, fine_dev=fine_dev, K=K, sub=sub, groups=Y // 2)
    TR = K // 2 // (Y + Z)
    most = max(Y, Z)
    vm = pltpu.VMEM
    chunk = (R, cap * W // LANES, LANES)

    def ar(width):
        return [
            vm((2, Y + Z, TR, width), F32),
            vm((Y + Z, TR, width), F32),
            vm((2, most - 1, TR, width), F32),
            vm((2, most, TR, width), F32),
            vm((2, Y + Z, TR, width), F32),
        ]

    dma = pltpu.SemaphoreType.DMA
    outs = pl.pallas_call(
        functools.partial(kernel, cfg),
        out_shape=(
            jax.ShapeDtypeStruct((K, W), F32),
            jax.ShapeDtypeStruct((fine_dev, W), F32),
            jax.ShapeDtypeStruct((n, W), BF16),
            jax.ShapeDtypeStruct((K // R, W), F32),
            jax.ShapeDtypeStruct((n,), F32),
        ),
        in_specs=[pl.BlockSpec(memory_space=vm)] * 4
        + [pl.BlockSpec(memory_space=pltpu.HBM)] * 2
        + [pl.BlockSpec(memory_space=vm)],
        out_specs=[pl.BlockSpec(memory_space=vm)] * 5,
        scratch_shapes=[
            vm(chunk, BF16),
            vm(chunk, BF16),
            vm((R, 1, 2 * cap * sub), F32),
            vm((R, 1, 2 * cap * sub), F32),
            vm(chunk, BF16),
            vm(chunk, BF16),
            *ar(W + LANES),
            *ar(W),
            vm((cfg["X"], 8, n), F32),
            vm((K, W), F32),
            vm((fine_dev, W), F32),
            dma((2,)),
            dma((5,)),
            dma((4,)),
            dma((1,)),
            dma((1,)),
            dma((16,)),
            dma((16,)),
            dma((1,)),
        ],
        compiler_params=pltpu.CompilerParams(
            collective_id=0, has_side_effects=True, vmem_limit_bytes=56 * 2**20
        ),
    )(
        embeddings,
        coarse_ids.reshape(1, n),
        fine_ids.reshape(1, n),
        pq_codes.T,
        old_coarse,
        old_fine,
        old_codebook,
    )
    return outs


def solution(mesh):
    devices = mesh.devices
    x = mesh.shape["rep"]
    chips = mesh.shape["rows"] // 2
    y = int(round(chips**0.5))
    z = chips // y
    torus = Mesh(devices.reshape(y, z, 2, x), (*ROWS, "rep"))
    cfg = {"Y": y, "Z": z, "C": 2, "X": x}
    return jax.shard_map(
        functools.partial(shards, cfg),
        mesh=torus,
        in_specs=(
            P(ROWS, "rep"),
            P(ROWS),
            P(ROWS),
            P(ROWS, "rep"),
            P(None, "rep"),
            P(ROWS, "rep"),
            P(ROWS, "rep"),
        ),
        out_specs=(P(None, "rep"), P(ROWS, "rep"), P(ROWS, "rep"), P(ROWS, "rep"), P(ROWS)),
        check_vma=False,
    )
```

```python
import functools

import jax
import jax.numpy as jnp
from jax import lax
from jax.experimental import pallas as pl
from jax.experimental.pallas import tpu as pltpu
from jax.sharding import Mesh
from jax.sharding import PartitionSpec as P

MESH = pl.DeviceIdType.MESH
ROWS = ("ry", "rz", "rc")
F32, BF16, I32 = jnp.float32, jnp.bfloat16, jnp.int32
LANES = 128


def iota(shape, dim):
    return lax.broadcasted_iota(I32, shape, dim)


def hot(cond):
    return jnp.where(cond, 1.0, 0.0).astype(BF16)


def dot(a, b):
    return jnp.dot(a, b, preferred_element_type=F32)


def parts(a, count):
    out = []
    for _ in range(count):
        p = a.astype(BF16)
        out.append(p)
        a = a - p.astype(F32)
    return out


def kernel(cfg, emb, cids, fids, pq, old_coarse, old_fine, old_book,
           o_coarse, o_fine, o_res, o_book, o_err,
           xs, xr, ms, mr, bs, br,
           in1, core1, rs1, x1, full1,
           in2, core2, rs2, x2, full2,
           err, coarse_old, fine_old, s_own, s_send, s_x, s_m, s_b, s_ar1, s_ar2, s_e):
    Y, Z, C, X = cfg["Y"], cfg["Z"], cfg["C"], cfg["X"]
    R, n, W, cap, fine_dev, K, sub = (cfg[k] for k in ("R", "n", "W", "cap", "fine_dev", "K", "sub"))
    S, half, TR, sw = R * cap, K // 2, K // 2 // (Y + Z), W // sub
    groups = cfg["groups"]
    src_g, slots_g = R // groups, S // groups
    y, z, c, x = (lax.axis_index(a) for a in (*ROWS, "rep"))

    def at(dy=0, dz=0, dc=0, dx=0):
        return {
            "ry": (y + dy) & (Y - 1),
            "rz": (z + dz) & (Z - 1),
            "rc": (c + dc) & (C - 1),
            "rep": (x + dx) & (X - 1),
        }

    zs = sorted(range(Z), key=lambda d: (min(d, Z - d), d))

    def pair(k, visit):
        first = isinstance(k, int) and k == 0
        for dz in zs:
            for dc in range(C):
                for side in range(2):
                    if first and side == dz == dc == 0:
                        continue
                    dy = (0, Y // 2)[side] if first else (k, Y - k)[side]
                    other = side if first else 1 - side
                    there = ((2 * k + side) * Z + dz) * C + dc
                    back = ((2 * k + other) * Z + (Z - dz) % Z) * C + (C - dc) % C
                    visit((dy, dz, dc), there, back)

    def peers(visit):
        pair(0, visit)

        def step(k, _):
            pair(k, visit)
            return 0

        if Y > 2:
            lax.fori_loop(1, Y // 2, step, 0)

    def remote(src, dst, recv, where, send):
        return pltpu.make_async_remote_copy(src, dst, send, recv, device_id=where, device_id_type=MESH)

    def arrived(ref, sem):
        pltpu.make_async_copy(ref, ref, sem).wait()

    gate = pltpu.get_barrier_semaphore()

    def greet(off, there, back):
        pl.semaphore_signal(gate, inc=1, device_id=at(*off), device_id_type=MESH)

    peers(greet)
    for d in range(1, X):
        pl.semaphore_signal(gate, inc=1, device_id=at(dx=d), device_id_type=MESH)

    fetches = [
        pltpu.make_async_copy(old_coarse, coarse_old, s_own.at[0]),
        pltpu.make_async_copy(old_fine, fine_old, s_own.at[1]),
    ]
    for f in fetches:
        f.start()

    cid_r, fid_r = cids[...], fids[...]
    own = fid_r // fine_dev
    loc = fid_r - own * fine_dev
    coarse_hot = hot(iota((K, n), 0) == cid_r)
    ones_lane = lambda lane: hot(iota((n, LANES), 1) == lane)
    pq_rows = pq[...].astype(F32)
    pq16 = jnp.transpose(jnp.concatenate([pq_rows] * (LANES // sub), axis=0))[:, :sub].astype(BF16)
    spread = hot((iota((sub, cap * sub), 1) & (sub - 1)) == iota((sub, cap * sub), 0))
    pq_wide = dot(pq16, spread)
    in1[:, :, :, :W] = dot(coarse_hot, emb[...]).reshape(2, Y + Z, TR, W)
    tally = dot(coarse_hot, ones_lane(sub))
    for m in range(sub):
        tally += dot(hot(iota((K, n), 0).astype(F32) == pq_rows[m : m + 1, :]), ones_lane(m))
    in1[:, :, :, W:] = tally.reshape(2, Y + Z, TR, LANES)

    turn = ((own // (Z * C)) - y) & (Y - 1)
    place_y = jnp.where(turn == 0, 0, jnp.where(turn == Y // 2, 1, jnp.where(turn < Y // 2, 2 * turn, 2 * (Y - turn) + 1)))
    rel_r = (
        place_y * (Z * C) + (((own // C) - z) & (Z - 1)) * C + ((own - c) & (C - 1))
    ).astype(F32)
    same = iota((n, n), 0) == iota((n, n), 1)

    def column(row):
        return jnp.sum(jnp.where(same, row, 0.0), axis=1, keepdims=True)

    rel_c, cid_c, loc_c = column(rel_r), column(cid_r.astype(F32)), column(loc.astype(F32))
    eq = rel_c == rel_r
    before = iota((n, n), 0) < iota((n, n), 1)
    after = iota((n, n), 0) > iota((n, n), 1)
    rank_r = jnp.sum(jnp.where(eq & before, 1.0, 0.0), axis=0, keepdims=True)
    rank_c = jnp.sum(jnp.where(eq & after, 1.0, 0.0), axis=1, keepdims=True)
    slot_r = rel_r * cap + rank_r
    slot_c = rel_c * cap + rank_c
    for g in range(groups):
        pick = hot((iota((slots_g, n), 0) + g * slots_g).astype(F32) == slot_r)
        rows = dot(pick, emb[...]).reshape(src_g, cap, W)
        xs[g * src_g : (g + 1) * src_g] = jnp.concatenate(
            [rows[:, :, w : w + LANES] for w in range(0, W, LANES)], axis=1
        ).astype(BF16)
    to_owner = hot(iota((R, n), 0).astype(F32) == rel_r)
    lane = iota((n, cap * sub), 1)
    slot_of_lane, field = (lane // sub).astype(F32), lane & (sub - 1)
    hi = jnp.floor(loc_c * (1.0 / 256.0))
    ids = jnp.where(field == 0, cid_c + 1.0, jnp.where(field == 1, loc_c - hi * 256.0, jnp.where(field == 2, hi + 1.0, 0.0)))
    mine = slot_of_lane == rank_c
    code_words = dot(to_owner, jnp.where(mine, pq_wide, 0.0).astype(BF16))
    id_words = dot(to_owner, jnp.where(mine, ids, 0.0).astype(BF16))
    ms[...] = jnp.concatenate([code_words, id_words], axis=1).reshape(R, 1, 2 * cap * sub)
    xr[0] = xs[0]
    mr[0] = ms[0]

    pl.semaphore_wait(gate, R - 1 + X - 1)

    def ar_core(inp, core, sems):
        remote(inp.at[1 - c], core, sems.at[0], at(dc=1), sems.at[8]).start()

    def ar_scatter(inp, core, rs, sems):
        arrived(core, sems.at[0])
        core[...] = core[...] + inp[c]
        for i in range(1, Y):
            remote(core.at[lax.rem(y + i, Y)], rs.at[0, i - 1], sems.at[1], at(dy=i), sems.at[9]).start()
        for i in range(1, Z):
            remote(core.at[Y + lax.rem(z + i, Z)], rs.at[1, i - 1], sems.at[2], at(dz=i), sems.at[10]).start()

    def ar_cross(core, rs, xx, sems):
        arrived(rs.at[0], sems.at[1])
        own_a = core[y] + jnp.sum(rs[0], axis=0)
        xx[0, z] = own_a
        for i in range(1, Z):
            remote(xx.at[0, z], xx.at[0, z], sems.at[3], at(dz=i), sems.at[11]).start()
        arrived(rs.at[1], sems.at[2])
        own_b = core[Y + z] + jnp.sum(rs[1], axis=0)
        xx[1, y] = own_b
        for i in range(1, Y):
            remote(xx.at[1, y], xx.at[1, y], sems.at[4], at(dy=i), sems.at[12]).start()

    def ar_gather(xx, full, sems, finish):
        arrived(rs_like(xx, Z), sems.at[3])
        full[c, y] = finish(jnp.sum(xx[0], axis=0), y)
        for i in range(1, Y):
            remote(full.at[c, y], full.at[c, y], sems.at[5], at(dy=i), sems.at[13]).start()
        arrived(rs_like(xx, Y), sems.at[4])
        full[c, Y + z] = finish(jnp.sum(xx[1], axis=0), Y + z)
        for i in range(1, Z):
            remote(full.at[c, Y + z], full.at[c, Y + z], sems.at[6], at(dz=i), sems.at[14]).start()

    def rs_like(xx, count):
        return xx.at[0, 0 : count - 1]

    def ar_pair(full, sems):
        arrived(full.at[0, 0 : Y - 1], sems.at[5])
        arrived(full.at[0, 0 : Z - 1], sems.at[6])
        remote(full.at[c], full.at[c], sems.at[7], at(dc=1), sems.at[15]).start()

    def ar_done(full, sems):
        arrived(full.at[0], sems.at[7])

    def ar_sent(inp, core, rs, xx, full, sems):
        arrived(core, sems.at[8])
        arrived(rs.at[0], sems.at[9])
        arrived(rs.at[1], sems.at[10])
        arrived(rs_like(xx, Z), sems.at[11])
        arrived(rs_like(xx, Y), sems.at[12])
        arrived(full.at[0, 0 : Y - 1], sems.at[13])
        arrived(full.at[0, 0 : Z - 1], sems.at[14])
        arrived(full.at[0], sems.at[15])

    def ship(g):
        def visit(off, i, d):
            remote(xs.at[d], xr.at[i], s_x.at[g], at(-off[0], -off[1], -off[2]), s_send.at[1]).start()

        if g < groups:
            pair(g, visit)

    def ship_words(g):
        def visit(off, i, d):
            remote(ms.at[d], mr.at[i], s_m.at[0], at(-off[0], -off[1], -off[2]), s_send.at[2]).start()

        if g < groups:
            pair(g, visit)

    def give(g):
        def visit(off, i, d):
            remote(bs.at[i], br.at[d], s_b.at[0], at(*off), s_send.at[3]).start()

        if g < groups:
            pair(g, visit)

    ar_core(in1, core1, s_ar1)
    ship(0)
    ar_scatter(in1, core1, rs1, s_ar1)
    ship(1)
    ship_words(0)
    ar_cross(core1, rs1, x1, s_ar1)
    ship(2)
    ship_words(1)
    fetches[0].wait()

    def coarse_mean(total, tile):
        first = pl.multiple_of(c * half + tile * TR, TR)
        count = total[:, W + sub : W + sub + 1]
        old = coarse_old[pl.ds(first, TR), :]
        mean = jnp.where(count > 0, total[:, :W] / jnp.maximum(count, 1.0), old)
        return jnp.concatenate([mean, total[:, W:]], axis=1)

    ar_gather(x1, full1, s_ar1, coarse_mean)
    ship(3)
    ship_words(2)
    ar_pair(full1, s_ar1)
    ship_words(3)

    def span(g):
        return slice(max(1, g * src_g), (g + 1) * src_g)

    arrived(mr.at[1:R], s_m.at[0])
    words = mr[...].reshape(R, 2 * cap * sub)
    code_w, id_w = words[:, : cap * sub], words[:, cap * sub :]
    by_src = hot((iota((S, R), 0) // cap) == iota((S, R), 1))
    mask_c = (iota((S, cap * sub), 1) // sub) == (iota((S, cap * sub), 0) & (cap - 1))
    pick_c = hot((iota((cap * sub, LANES), 0) & (sub - 1)) == iota((cap * sub, LANES), 1))
    id_c = dot(jnp.where(mask_c, dot(by_src, id_w.astype(BF16)), 0.0).astype(BF16), pick_c)
    by_src_t = hot((iota((R, S), 1) // cap) == iota((R, S), 0))
    mask_r = (iota((cap * sub, S), 0) // sub) == (iota((cap * sub, S), 1) & (cap - 1))
    pick_r = hot((iota((sub, cap * sub), 1) & (sub - 1)) == iota((sub, cap * sub), 0))

    def along_lanes(w):
        wide = dot(jnp.transpose(w).astype(BF16), by_src_t)
        return dot(pick_r, jnp.where(mask_r, wide, 0.0).astype(BF16))

    id_r, code_r = along_lanes(id_w), along_lanes(code_w)
    cid_slot = id_c[:, 0:1] - 1.0
    fid_slot = (id_c[:, 2:3] - 1.0) * 256.0 + id_c[:, 1:2]
    fid_lane = (id_r[2:3, :] - 1.0) * 256.0 + id_r[1:2, :]

    ar_done(full1, s_ar1)
    table = full1[...].reshape(K, W + LANES)
    o_coarse[...] = table[:, :W]
    coarse_parts = parts(table[:, :W], 3)

    fine_sum = jnp.zeros((fine_dev, W), F32)
    fine_count = jnp.zeros((fine_dev, 1), F32)
    for g in range(groups):
        arrived(xr.at[span(g)], s_x.at[g])
        lo = g * slots_g
        got = xr[g * src_g : (g + 1) * src_g].astype(F32)
        got = jnp.concatenate(
            [got[:, w * cap : (w + 1) * cap].reshape(slots_g, LANES) for w in range(W // LANES)], axis=1
        )
        c_hot = hot(iota((slots_g, K), 1).astype(F32) == cid_slot[lo : lo + slots_g])
        base = sum(dot(c_hot, p) for p in coarse_parts)
        cr = (got - base).astype(BF16)
        f_hot = iota((fine_dev, slots_g), 0).astype(F32) == fid_lane[:, lo : lo + slots_g]
        fine_sum += dot(hot(f_hot), cr)
        fine_count += jnp.sum(jnp.where(f_hot, 1.0, 0.0), axis=1, keepdims=True)
        cr_rows = cr.astype(F32).reshape(src_g, cap, W)
        xr[g * src_g : (g + 1) * src_g] = jnp.concatenate(
            [cr_rows[:, :, w : w + LANES] for w in range(0, W, LANES)], axis=1
        ).astype(BF16)
    fetches[1].wait()
    new_fine = jnp.where(fine_count > 0, fine_sum / jnp.maximum(fine_count, 1.0), fine_old[...])
    o_fine[...] = new_fine
    fine_parts = parts(new_fine, 2)

    col = iota((1, W), 1) // sw
    code_sum = jnp.zeros((K, W), F32)
    for g in range(groups):
        lo = g * slots_g
        cr = xr[g * src_g : (g + 1) * src_g].astype(F32)
        cr = jnp.concatenate(
            [cr[:, w * cap : (w + 1) * cap].reshape(slots_g, LANES) for w in range(W // LANES)], axis=1
        )
        f_hot = hot(iota((slots_g, fine_dev), 1).astype(F32) == fid_slot[lo : lo + slots_g])
        res = (cr - sum(dot(f_hot, p) for p in fine_parts)).astype(BF16)
        res32 = res.astype(F32)
        res_rows = res32.reshape(src_g, cap, W)
        bs[g * src_g : (g + 1) * src_g] = jnp.concatenate(
            [res_rows[:, :, w : w + LANES] for w in range(0, W, LANES)], axis=1
        ).astype(BF16)

        for m in range(sub):
            k_hot = hot(iota((K, slots_g), 0).astype(F32) == code_r[m : m + 1, lo : lo + slots_g])
            code_sum += jnp.where(col == m, dot(k_hot, res), 0.0)
    in2[...] = code_sum.reshape(2, Y + Z, TR, W)
    ar_core(in2, core2, s_ar2)
    br[0] = bs[0]

    counts = table[:, W:]
    widen = hot(iota((LANES, W), 1) // sw == iota((LANES, W), 0))
    count_wide = sum(dot(p, widen) for p in parts(counts, 2))

    give(0)
    ar_scatter(in2, core2, rs2, s_ar2)
    give(1)
    ar_cross(core2, rs2, x2, s_ar2)
    give(2)
    ar_gather(x2, full2, s_ar2, lambda total, tile: total)
    give(3)
    ar_pair(full2, s_ar2)

    arrived(br.at[1:R], s_b.at[0])
    rows = br[...].astype(F32)
    rows = jnp.concatenate([rows[:, w * cap : (w + 1) * cap].reshape(S, LANES) for w in range(W // LANES)], axis=1)
    fetch = hot(iota((n, S), 1).astype(F32) == slot_c)
    res = dot(fetch, rows.astype(BF16))
    o_res[...] = res.astype(BF16)

    ar_done(full2, s_ar2)
    book = full2[...].reshape(K, W) / jnp.maximum(count_wide, 1.0)
    share = K // R
    me = (y * Z + z) * C + c
    tall = max(8, share)
    take = hot(iota((tall, K), 1) == iota((tall, K), 0) + me * share)
    own_book = sum(dot(take, p) for p in parts(book, 3))
    own_count = sum(dot(take, p) for p in parts(count_wide, 2))
    o_book[...] = jnp.where(own_count[:share] > 0, own_book[:share], old_book[...])
    book_parts = parts(book, 2)
    rebuilt = jnp.zeros((n, W), F32)
    for m in range(sub):
        k_hot = hot(iota((n, K), 1).astype(F32) == pq16[:, m : m + 1].astype(F32))
        rebuilt = jnp.where(col == m, sum(dot(k_hot, p) for p in book_parts), rebuilt)
    differ = res - rebuilt
    error = jnp.sum(differ * differ, axis=1, keepdims=True)
    error_row = jnp.sum(jnp.where(same, error, 0.0), axis=0, keepdims=True)
    err[x] = jnp.broadcast_to(error_row, (8, n))
    for d in range(1, X):
        remote(err.at[x], err.at[x], s_e.at[0], at(dx=d), s_send.at[4]).start()
    if X > 1:
        arrived(err.at[0 : X - 1], s_e.at[0])
    o_err[...] = (jnp.sum(err[...], axis=0)[:1] * (1.0 / (W * X))).reshape(n)

    if X > 1:
        arrived(err.at[0 : X - 1], s_send.at[4])
    arrived(xr.at[1:R], s_send.at[1])
    arrived(mr.at[1:R], s_send.at[2])
    arrived(br.at[1:R], s_send.at[3])
    ar_sent(in1, core1, rs1, x1, full1, s_ar1)
    ar_sent(in2, core2, rs2, x2, full2, s_ar2)


def shards(cfg, embeddings, coarse_ids, fine_ids, pq_codes, old_coarse, old_fine, old_codebook):
    n, W = embeddings.shape
    K, fine_dev, sub = old_coarse.shape[0], old_fine.shape[0], pq_codes.shape[1]
    Y, Z = cfg["Y"], cfg["Z"]
    R = Y * Z * cfg["C"]
    cap = 4 * n // R
    cfg = dict(cfg, R=R, n=n, W=W, cap=cap, fine_dev=fine_dev, K=K, sub=sub, groups=Y // 2)
    TR = K // 2 // (Y + Z)
    most = max(Y, Z)
    vm = pltpu.VMEM
    chunk = (R, cap * W // LANES, LANES)

    def ar(width):
        return [
            vm((2, Y + Z, TR, width), F32),
            vm((Y + Z, TR, width), F32),
            vm((2, most - 1, TR, width), F32),
            vm((2, most, TR, width), F32),
            vm((2, Y + Z, TR, width), F32),
        ]

    dma = pltpu.SemaphoreType.DMA
    outs = pl.pallas_call(
        functools.partial(kernel, cfg),
        out_shape=(
            jax.ShapeDtypeStruct((K, W), F32),
            jax.ShapeDtypeStruct((fine_dev, W), F32),
            jax.ShapeDtypeStruct((n, W), BF16),
            jax.ShapeDtypeStruct((K // R, W), F32),
            jax.ShapeDtypeStruct((n,), F32),
        ),
        in_specs=[pl.BlockSpec(memory_space=vm)] * 4
        + [pl.BlockSpec(memory_space=pltpu.HBM)] * 2
        + [pl.BlockSpec(memory_space=vm)],
        out_specs=[pl.BlockSpec(memory_space=vm)] * 5,
        scratch_shapes=[
            vm(chunk, BF16),
            vm(chunk, BF16),
            vm((R, 1, 2 * cap * sub), F32),
            vm((R, 1, 2 * cap * sub), F32),
            vm(chunk, BF16),
            vm(chunk, BF16),
            *ar(W + LANES),
            *ar(W),
            vm((cfg["X"], 8, n), F32),
            vm((K, W), F32),
            vm((fine_dev, W), F32),
            dma((2,)),
            dma((5,)),
            dma((4,)),
            dma((1,)),
            dma((1,)),
            dma((16,)),
            dma((16,)),
            dma((1,)),
        ],
        compiler_params=pltpu.CompilerParams(
            collective_id=0, has_side_effects=True, vmem_limit_bytes=56 * 2**20
        ),
    )(
        embeddings,
        coarse_ids.reshape(1, n),
        fine_ids.reshape(1, n),
        pq_codes.T,
        old_coarse,
        old_fine,
        old_codebook,
    )
    return outs


def solution(mesh):
    devices = mesh.devices
    x = mesh.shape["rep"]
    chips = mesh.shape["rows"] // 2
    y = int(round(chips**0.5))
    z = chips // y
    torus = Mesh(devices.reshape(y, z, 2, x), (*ROWS, "rep"))
    cfg = {"Y": y, "Z": z, "C": 2, "X": x}
    return jax.shard_map(
        functools.partial(shards, cfg),
        mesh=torus,
        in_specs=(
            P(ROWS, "rep"),
            P(ROWS),
            P(ROWS),
            P(ROWS, "rep"),
            P(None, "rep"),
            P(ROWS, "rep"),
            P(ROWS, "rep"),
        ),
        out_specs=(P(None, "rep"), P(ROWS, "rep"), P(ROWS, "rep"), P(ROWS, "rep"), P(ROWS)),
        check_vma=False,
    )
```
